256 devices in a mesh: seq: 32 (over z, y_lo, core), mp: 8 (over x, y_hi).
Axes of the slice: x: 4, y: 4 (y_hi: 2, y_lo: 2; y = y_hi * 2 + y_lo), z: 8, core: 2. Of those that a mesh axis runs over, the one named last changes fastest.
Arguments:
- frames: bfloat16 [262144, 1024], P(('seq', 'mp')), may hold values from -6 to 6
- conv_kernel: float32 [31, 1024], replicated, may hold values from -1 to 1
- key_weight: bfloat16 [1024, 1024], P(None, 'mp'), may hold values from -0.1875 to 0.1875
- value_weight: bfloat16 [1024, 1024], P(None, 'mp'), may hold values from -0.1875 to 0.1875
- queries: bfloat16 [65536, 1024], P(('seq', 'mp')), may hold values from -512 to 512
- offsets: int32 [65536], P(('seq', 'mp')), may hold values from 0 to 261888, as said below
Outputs:
- context: bfloat16 [65536, 1024], P(('seq', 'mp'))
The draws below stay inside these ranges and needn't reach their ends.
Inputs may be any that keep to these rules, and one draw needn't show every extreme that they name: offsets never fall; for the token at position t and i = t // 256, its band lies within frames i * 1024 - 512 to (i + 1) * 1024 + 511.
All inputs are finite; a program needn't handle non-finite values.
Results may differ from the reference program's by a relative error of at most 0.0075.
The reference program's roundings to bfloat16 on the way count: a program that leaves them out, or rounds other values in their place, can miss the bound.
Values may be sent and summed in bfloat16 or wider, within the bound.
A program may use at most 64 MiB of HBM per device.

```python
import jax
import jax.numpy as jnp
from jax import lax

DE = 1024
HEADS = 16
HEAD_DIM = 64
KW = 31
BAND = 256
FR_DEV = 1024
TOK_DEV = 256
D = 1024
FRAMES = 262144
TOKENS = 65536


def draw_queries(key, part):
    key = jax.random.fold_in(key, 11)
    first_key = jax.random.fold_in(key, 0)
    normal_values = jax.random.normal(first_key, (TOKENS, D), jnp.float32)
    return jnp.clip(normal_values, -512.0, 512.0).astype(jnp.bfloat16)


def draw_offsets(key, part):
    key = jax.random.fold_in(key, 7)
    first_key, second_key = jax.random.split(key)
    position = jnp.arange(TOKENS, dtype=jnp.int32)
    nominal = position // TOK_DEV * FR_DEV + position % TOK_DEV * FR_DEV // TOK_DEV
    jitter = jax.random.randint(first_key, (TOKENS,), -(FR_DEV // 4), FR_DEV // 4)
    aligned = nominal - BAND // 2 + jitter
    chosen = jax.random.randint(second_key, (), 0, TOKENS // TOK_DEV - 1)
    forced_at = (chosen + 1) * TOK_DEV - 1
    aligned = jnp.where(position == forced_at, (chosen + 1) * FR_DEV + FR_DEV // 2 - BAND, aligned)
    aligned = lax.cummax(aligned, axis=0)
    aligned = jnp.clip(aligned, 0, FRAMES - BAND)
    return jnp.where(position == TOKENS - 1, FRAMES - BAND, aligned).astype(jnp.int32)


def levels(key, extent, pieces, smallest, largest):
    factor_of, own = 1.0, jax.random.fold_in(key, 6)
    for dim, shards_of in pieces:
        steps = jnp.exp(jax.random.uniform(jax.random.fold_in(own, dim), (shards_of,), jnp.float32, smallest / len(pieces), largest / len(pieces)))
        factor_of = factor_of * jnp.repeat(steps, extent[dim] // shards_of).reshape([-1 if axis == dim else 1 for axis in range(len(extent))])
    return factor_of


def scatter_about(rng, extent, width, limit, cuts=(), held_as=jnp.bfloat16):
    factor_of = levels(rng, extent, cuts, -0.22, 0.18) if cuts else 1.0
    result = jax.random.normal(rng, extent, jnp.float32) * width * factor_of
    return jnp.minimum(jnp.maximum(result, -limit), limit).astype(held_as)


def setup_inputs(seed: int = 0) -> dict:
    key_list = jax.random.split(jax.random.key(seed), 7)
    return {
        "frames": scatter_about(key_list[0], (FRAMES, DE), 1.0, 6.0, ((0, 256),)),
        "conv_kernel": scatter_about(key_list[1], (KW, DE), KW ** -0.5, 1.0, (), jnp.float32),
        "key_weight": scatter_about(key_list[2], (DE, D), DE ** -0.5, 0.1875, ((1, 8),)),
        "value_weight": scatter_about(key_list[3], (DE, D), DE ** -0.5, 0.1875, ((1, 8),)),
        "queries": draw_queries(jax.random.fold_in(key_list[6], 71), 0),
        "offsets": draw_offsets(jax.random.fold_in(key_list[6], 71), 0),
    }


def reference(frames, conv_kernel, key_weight, value_weight, queries, offsets):
    rim_width = (KW - 1) // 2
    padded = jnp.pad(frames.astype(jnp.float32), ((rim_width, rim_width), (0, 0)))
    mixed = jnp.zeros((FRAMES, DE), jnp.float32)
    for offset_tap in range(KW):
        mixed = mixed + conv_kernel[offset_tap] * padded[offset_tap:offset_tap + FRAMES]
    encoded = (frames.astype(jnp.float32) + jax.nn.silu(mixed)).astype(jnp.bfloat16)

    def project_block(rows_block):
        keys_block = jnp.dot(rows_block, key_weight, preferred_element_type=jnp.float32).astype(jnp.bfloat16)
        values_block = jnp.dot(rows_block, value_weight, preferred_element_type=jnp.float32).astype(jnp.bfloat16)
        return keys_block, values_block

    keys_all, values_all = lax.map(project_block, encoded.reshape(FRAMES // FR_DEV, FR_DEV, DE))
    keys_all = keys_all.reshape(FRAMES, D)
    values_all = values_all.reshape(FRAMES, D)
    block_rows = min(64, TOKENS)
    score_scale = HEAD_DIM ** -0.5

    def attend_block(pair):
        query_block, offset_block = pair
        band_rows = offset_block[:, None] + jnp.arange(BAND, dtype=jnp.int32)[None, :]
        band_keys = keys_all[band_rows].astype(jnp.float32).reshape(block_rows, BAND, HEADS, HEAD_DIM)
        band_values = values_all[band_rows].astype(jnp.float32).reshape(block_rows, BAND, HEADS, HEAD_DIM)
        query_heads = query_block.astype(jnp.float32).reshape(block_rows, HEADS, HEAD_DIM)
        scores = jnp.einsum("thd,tbhd->thb", query_heads, band_keys) * score_scale
        peak_score = jnp.max(scores, axis=2, keepdims=True)
        weights = jnp.exp(scores - peak_score)
        row_total = jnp.sum(weights, axis=2, keepdims=True)
        probability = (weights / row_total).astype(jnp.bfloat16)
        mixed_heads = jnp.einsum("thb,tbhd->thd", probability.astype(jnp.float32), band_values)
        return mixed_heads.reshape(block_rows, D).astype(jnp.bfloat16)

    context = lax.map(attend_block, (queries.reshape(-1, block_rows, D), offsets.reshape(-1, block_rows)))
    return context.reshape(TOKENS, D)
```

```python
import jax
import jax.numpy as jnp
from jax import lax
from jax.experimental import pallas as pl
from jax.experimental.pallas import tpu as pltpu
from jax.sharding import PartitionSpec as P

BF = jnp.bfloat16
F32 = jnp.float32
MESH = pl.DeviceIdType.MESH

HEAD_DIM = 64
BAND = 256
ROWS = 1024
TOKS = 256
WIDTH = 1024
LANES = 128
BLOCKS = WIDTH // LANES
TAPS = 31
HALF = ROWS // 2
HALO = 16
TILE = 128
PACK = LANES + 16
CHUNKS = 4
CCOLS = WIDTH // CHUNKS
NEG = -1e30
SCALE2 = HEAD_DIM ** -0.5 * 1.4426950408889634
MERGE_LAG = 2


def kernel(
    frames, taps, key_panel, value_panel, queries, offs,
    out,
    xpad, enc, wbuf, kbuf, vbuf, hbuf, offown, offn, qn, bias, biasn,
    part, oret, osend, pret, msend, ctx, stat,
    halo_s, halo_r, off_s, off_r, q_s, q_r, f_s, f_r,
    w_s, w_r, b_s, b_r, o_s, o_r, p_s, p_r,
):
    seq, mp = lax.axis_index("seq"), lax.axis_index("mp")
    me = seq * 8 + mp
    x, hi = mp // 2, mp % 2
    core, lo = seq % 2, (seq // 2) % 2
    sign = 1 - 2 * hi

    def at(index):
        wrapped = lax.rem(index + 256, 256)
        return {"seq": wrapped // 8, "mp": lax.rem(wrapped, 8)}

    up, down = at(me + 1), at(me - 1)
    partner = {"seq": seq, "mp": mp + sign}
    other = at(me - sign)
    onward = at(me + 2 * sign)
    source = at(me - 2 * sign)
    sibling = {"seq": seq + 1 - 2 * core, "mp": mp}
    across = {"seq": seq + 2 - 4 * lo, "mp": mp + sign}
    xplus = {"seq": seq, "mp": lax.rem(mp + 2, 8)}
    xminus = {"seq": seq, "mp": lax.rem(mp + 6, 8)}
    relay = {"seq": seq, "mp": lax.rem(mp + 6 + 4 * hi, 8)}

    def copy(src, dst, send, recv, device):
        return pltpu.make_async_remote_copy(
            src_ref=src, dst_ref=dst, send_sem=send, recv_sem=recv, device_id=device, device_id_type=MESH
        )

    def panel_of(r):
        g = r // 2
        step = g + (g // 2) * (5 - 2 * g)
        flip = lax.rem(r + hi, 2)
        return lax.rem(x + step, 4) * 2 + flip

    slot_p, slot_o = 1 - hi, hi

    halo_up = copy(frames.at[pl.ds(ROWS - HALO, HALO)], hbuf.at[0], halo_s.at[0], halo_r.at[0], up)
    halo_down = copy(frames.at[pl.ds(0, HALO)], hbuf.at[1], halo_s.at[1], halo_r.at[1], down)
    off_p = copy(offown, offn.at[hi], off_s.at[0], off_r.at[hi], partner)
    off_o = copy(offown, offn.at[1 - hi], off_s.at[1], off_r.at[1 - hi], other)

    def q_copy(c):
        cols = pl.ds(c * CCOLS, CCOLS)
        return copy(queries.at[:, cols], qn.at[hi, :, cols], q_s.at[c], q_r.at[c], partner)

    def q_arrival(c):
        cols = pl.ds(c * CCOLS, CCOLS)
        dst = qn.at[slot_p, :, cols]
        return copy(dst, dst, q_s.at[c], q_r.at[c], partner)

    def f_copy(c):
        cols = pl.ds(c * CCOLS, CCOLS)
        return copy(qn.at[slot_p, :, cols], qn.at[hi, :, cols], f_s.at[c], f_r.at[c], onward)

    def f_arrival(c):
        cols = pl.ds(c * CCOLS, CCOLS)
        dst = qn.at[slot_o, :, cols]
        return copy(dst, dst, f_s.at[c], f_r.at[c], source)

    def w_copy(n, src, dst, device):
        return copy(wbuf.at[src, core], wbuf.at[dst, core], w_s.at[n], w_r.at[dst], device)

    own_across = w_copy(0, 0, 1, across)
    own_xplus = w_copy(1, 0, 4, xplus)
    own_xminus = w_copy(2, 0, 2, xminus)
    next_xplus = w_copy(3, 1, 5, xplus)
    next_xminus = w_copy(4, 1, 3, xminus)
    relay_own = w_copy(5, 2 + 2 * hi, 6, relay)
    relay_next = w_copy(6, 3 + 2 * hi, 7, relay)

    def w_arrival(r):
        dst = wbuf.at[r, core]
        return copy(dst, dst, w_s.at[0], w_r.at[r], across)

    def b_copy(r):
        return copy(wbuf.at[r, core], wbuf.at[r, core], b_s.at[r], b_r.at[r], sibling)

    def b_arrival(r):
        dst = wbuf.at[r, 1 - core]
        return copy(dst, dst, b_s.at[r], b_r.at[r], sibling)

    def o_copy(a):
        return copy(osend.at[a], oret.at[a], o_s.at[a], o_r.at[a], source)

    def p_copy(a):
        return copy(msend.at[a], pret.at[a], p_s.at[a], p_r.at[a], partner)

    barrier = pltpu.get_barrier_semaphore()
    greeted = (up, down, onward, source, sibling, across, xplus, xminus)
    for device in greeted:
        pl.semaphore_signal(barrier, inc=1, device_id=device, device_id_type=MESH)
    offown[...] = jnp.broadcast_to(offs[...], (8, TOKS))
    wbuf[0, 0] = key_panel[...]
    wbuf[0, 1] = value_panel[...]
    pl.semaphore_wait(barrier, len(greeted))

    halo_up.start()
    halo_down.start()
    own_across.start()
    off_p.start()
    off_o.start()
    own_xplus.start()
    own_xminus.start()
    for c in range(CHUNKS):
        q_copy(c).start()

    def band_bias(ref, first, row):
        count = ref.shape[0]

        def fill(n, _):
            rows = pl.ds(pl.multiple_of(n * 128, 128), 128)
            frame = first + n * 128 + lax.broadcasted_iota(jnp.int32, (128, TOKS), 0)
            gap = frame - row
            ref[rows, :] = jnp.where((gap & -BAND) == 0, 0.0, NEG)
            return 0

        lax.fori_loop(0, count // 128, fill, 0)

    band_bias(bias, me * ROWS, offown[0:1, :])

    halo_up.wait_recv()
    halo_down.wait_recv()

    def after_block(b):
        @pl.when(b == 1)
        def _():
            q_arrival(0).wait_recv()
            f_copy(0).start()

        @pl.when(b == 3)
        def _():
            w_arrival(1).wait_recv()
            next_xplus.start()
            next_xminus.start()
            b_copy(1).start()
            q_arrival(1).wait_recv()
            f_copy(1).start()

        @pl.when(b == 4)
        def _():
            w_arrival(2).wait_recv()
            b_copy(2).start()
            w_arrival(4).wait_recv()
            b_copy(4).start()
            relay_own.start()

        @pl.when(b == 5)
        def _():
            q_arrival(2).wait_recv()
            f_copy(2).start()

        @pl.when(b == 7)
        def _():
            q_arrival(3).wait_recv()
            f_copy(3).start()
            w_arrival(3).wait_recv()
            b_copy(3).start()
            w_arrival(5).wait_recv()
            b_copy(5).start()
            relay_next.start()

    def conv_block(b, _):
        cols = pl.ds(pl.multiple_of(b * LANES, LANES), LANES)
        xpad[pl.ds(0, HALO), :] = jnp.where(me > 0, hbuf[0, :, cols].astype(F32), 0.0)
        xpad[pl.ds(HALO, ROWS), :] = frames[:, cols].astype(F32)
        xpad[pl.ds(HALO + ROWS, HALO), :] = jnp.where(me < 255, hbuf[1, :, cols].astype(F32), 0.0)

        def tile(t, _):
            top = pl.multiple_of(t * TILE, TILE)
            acc = jnp.zeros((TILE, LANES), F32)
            for phase in range(8):
                window = xpad[pl.ds(top + phase + 1, TILE + 24), :]
                for k in range(phase, TAPS, 8):
                    acc = acc + taps[pl.ds(k, 1), cols] * window[k - phase : k - phase + TILE]
            here = xpad[pl.ds(top + HALO, TILE), :]
            half = 0.5 * acc
            enc[pl.ds(top, TILE), cols] = (here + (half + half * jnp.tanh(half))).astype(BF)
            return 0

        lax.fori_loop(0, ROWS // TILE, tile, 0)
        after_block(b)
        return 0

    lax.fori_loop(0, BLOCKS, conv_block, 0)

    def project(r, _):
        @pl.when(r == 2)
        def _():
            w_arrival(6).wait_recv()
            b_copy(6).start()

        @pl.when(r == 4)
        def _():
            w_arrival(7).wait_recv()
            b_copy(7).start()

        @pl.when(r > 0)
        def _():
            b_arrival(r).wait_recv()

        a = panel_of(r)

        def rows_part(n, _):
            rows = pl.ds(pl.multiple_of(n * HALF, HALF), HALF)
            weight = jnp.concatenate([wbuf[r, 0], wbuf[r, 1]], axis=1)
            both = jnp.dot(enc[rows, :], weight, preferred_element_type=F32)
            kbuf[a, rows, :] = both[:, :LANES].astype(BF)
            vbuf[a, :, rows] = both[:, LANES:].T.astype(BF)
            return 0

        lax.fori_loop(0, 2, rows_part, 0)
        return 0

    lax.fori_loop(0, BLOCKS, project, 0)

    lane = lax.broadcasted_iota(jnp.int32, (TOKS, LANES), 1)

    def attend(q, keys, values_t, mask):
        result = []
        for h in range(2):
            inside = (lane >= h * HEAD_DIM) & (lane < (h + 1) * HEAD_DIM)
            masked_q = jnp.where(inside, q.astype(F32), 0.0).astype(BF)
            scores = lax.dot_general(
                keys, masked_q, (((1,), (1,)), ((), ())), preferred_element_type=F32
            ) + mask
            peak = jnp.max(scores, axis=0, keepdims=True)
            weights = jnp.exp2((scores - peak) * SCALE2)
            total = jnp.sum(weights, axis=0, keepdims=True)
            mixed = jnp.dot(
                values_t[h * HEAD_DIM : (h + 1) * HEAD_DIM], weights.astype(BF), preferred_element_type=F32
            )
            result.append((mixed, peak, total))
        return result

    def three(v):
        first = v.astype(BF).astype(F32)
        second = (v - first).astype(BF).astype(F32)
        return [first, second, (v - first) - second]

    def attend_remote(a, slot, target):
        cols = pl.ds(pl.multiple_of(a * LANES, LANES), LANES)
        part_rows = pl.ds(pl.multiple_of(slot * HALF, HALF), HALF)
        heads = attend(qn[slot, :, cols], kbuf[a, part_rows, :], vbuf[a, :, part_rows], biasn[slot])
        rows = []
        for h, (mixed, peak, total) in enumerate(heads):
            target[a, h * HEAD_DIM : (h + 1) * HEAD_DIM, :] = (mixed / total).astype(BF)
            rows += three(peak) + three(total)
        rows.append(jnp.zeros((4, TOKS), F32))
        target[a, LANES:, :] = jnp.concatenate(rows, axis=0).astype(BF)

    def merge(a):
        o_copy(a).wait_recv()
        theirs = oret[a].astype(F32)
        mine = part[a].astype(F32)
        msend[a] = jnp.where(theirs[LANES : LANES + 1] > 0.1 * NEG, theirs, mine).astype(BF)
        p_copy(a).start()

    for slot in range(2):
        copy(offn.at[slot], offn.at[slot], off_s.at[slot], off_r.at[slot], partner).wait_recv()
        band_bias(biasn.at[slot], me * ROWS + slot * HALF, offn[slot, 0:1, :])

    def remote_step(a, _):
        @pl.when(a % 2 == 0)
        def _():
            f_arrival(a // 2).wait_recv()

        attend_remote(a, slot_o, osend)
        o_copy(a).start()
        attend_remote(a, slot_p, part)

        @pl.when(a >= MERGE_LAG)
        def _():
            merge(a - MERGE_LAG)

        return 0

    lax.fori_loop(0, BLOCKS, remote_step, 0)

    def own_step(a, _):
        cols = pl.ds(pl.multiple_of(a * LANES, LANES), LANES)
        heads = attend(queries[:, cols], kbuf[a], vbuf[a], bias[...])
        rows = []
        for h, (mixed, peak, total) in enumerate(heads):
            ctx[a, h * HEAD_DIM : (h + 1) * HEAD_DIM, :] = mixed
            rows += [peak, total]
        rows.append(jnp.zeros((4, TOKS), F32))
        stat[a] = jnp.concatenate(rows, axis=0)

        @pl.when(a < MERGE_LAG)
        def _():
            merge(a + BLOCKS - MERGE_LAG)

        return 0

    lax.fori_loop(0, BLOCKS, own_step, 0)

    def final_step(a, _):
        cols = pl.ds(pl.multiple_of(a * LANES, LANES), LANES)
        p_copy(a).wait_recv()
        far_rows = pret[a, LANES:, :].astype(F32)
        parts = []
        for h in range(2):
            far_peak = far_rows[6 * h : 6 * h + 1] + far_rows[6 * h + 1 : 6 * h + 2] + far_rows[6 * h + 2 : 6 * h + 3]
            far_total = far_rows[6 * h + 3 : 6 * h + 4] + far_rows[6 * h + 4 : 6 * h + 5] + far_rows[6 * h + 5 : 6 * h + 6]
            peak, total = stat[a, 2 * h : 2 * h + 1, :], stat[a, 2 * h + 1 : 2 * h + 2, :]
            top = jnp.maximum(peak, far_peak)
            near_weight = jnp.exp2((peak - top) * SCALE2)
            far_weight = jnp.exp2((far_peak - top) * SCALE2) * far_total
            scale = 1.0 / (near_weight * total + far_weight)
            head_rows = slice(h * HEAD_DIM, (h + 1) * HEAD_DIM)
            parts.append(
                ctx[a, head_rows, :] * (near_weight * scale) + pret[a, head_rows, :].astype(F32) * (far_weight * scale)
            )
        out[:, cols] = jnp.concatenate(parts, axis=0).T.astype(BF)
        return 0

    lax.fori_loop(0, BLOCKS, final_step, 0)

    for sent in (
        halo_up, halo_down, off_p, off_o, own_across, own_xplus, own_xminus,
        next_xplus, next_xminus, relay_own, relay_next,
    ):
        sent.wait_send()
    for c in range(CHUNKS):
        q_copy(c).wait_send()
        f_copy(c).wait_send()

    def drain(a, _):
        o_copy(a).wait_send()
        p_copy(a).wait_send()

        @pl.when(a > 0)
        def _():
            b_copy(a).wait_send()

        return 0

    lax.fori_loop(0, BLOCKS, drain, 0)


def shards(frames, conv_kernel, key_weight, value_weight, queries, offsets):
    dma = pltpu.SemaphoreType.DMA
    whole = pl.BlockSpec(memory_space=pltpu.VMEM)
    return pl.pallas_call(
        kernel,
        out_shape=jax.ShapeDtypeStruct((TOKS, WIDTH), BF),
        in_specs=[whole] * 6,
        out_specs=whole,
        scratch_shapes=[
            pltpu.VMEM((ROWS + 2 * HALO + 8, LANES), F32),
            pltpu.VMEM((ROWS, WIDTH), BF),
            pltpu.VMEM((BLOCKS, 2, WIDTH, LANES), BF),
            pltpu.VMEM((BLOCKS, ROWS, LANES), BF),
            pltpu.VMEM((BLOCKS, LANES, ROWS), BF),
            pltpu.VMEM((2, HALO, WIDTH), BF),
            pltpu.VMEM((8, TOKS), jnp.int32),
            pltpu.VMEM((2, 8, TOKS), jnp.int32),
            pltpu.VMEM((2, TOKS, WIDTH), BF),
            pltpu.VMEM((ROWS, TOKS), F32),
            pltpu.VMEM((2, HALF, TOKS), F32),
            pltpu.VMEM((BLOCKS, PACK, TOKS), BF),
            pltpu.VMEM((BLOCKS, PACK, TOKS), BF),
            pltpu.VMEM((BLOCKS, PACK, TOKS), BF),
            pltpu.VMEM((BLOCKS, PACK, TOKS), BF),
            pltpu.VMEM((BLOCKS, PACK, TOKS), BF),
            pltpu.VMEM((BLOCKS, LANES, TOKS), F32),
            pltpu.VMEM((BLOCKS, 8, TOKS), F32),
            dma((2,)), dma((2,)), dma((2,)), dma((2,)),
            dma((CHUNKS,)), dma((CHUNKS,)), dma((CHUNKS,)), dma((CHUNKS,)),
            dma((7,)), dma((8,)), dma((8,)), dma((8,)),
            dma((BLOCKS,)), dma((BLOCKS,)), dma((BLOCKS,)), dma((BLOCKS,)),
        ],
        compiler_params=pltpu.CompilerParams(
            collective_id=0, has_side_effects=True, vmem_limit_bytes=48 * 1024 * 1024
        ),
        cost_estimate=pl.CostEstimate(
            flops=9_000_000_000, bytes_accessed=4_500_000, transcendentals=10_000_000
        ),
        name="speech_window",
    )(frames, conv_kernel, key_weight, value_weight, queries, offsets.reshape(1, TOKS))


def solution(mesh):
    return jax.shard_map(
        shards,
        mesh=mesh,
        in_specs=(
            P(("seq", "mp"), None),
            P(),
            P(None, "mp"),
            P(None, "mp"),
            P(("seq", "mp"), None),
            P(("seq", "mp")),
        ),
        out_specs=P(("seq", "mp"), None),
        check_vma=False,
    )
```

```python
import jax
import jax.numpy as jnp
from jax import lax
from jax.experimental import pallas as pl
from jax.experimental.pallas import tpu as pltpu
from jax.sharding import PartitionSpec as P

BF = jnp.bfloat16
F32 = jnp.float32
MESH = pl.DeviceIdType.MESH

HEAD_DIM = 64
BAND = 256
ROWS = 1024
TOKS = 256
WIDTH = 1024
LANES = 128
BLOCKS = WIDTH // LANES
TAPS = 31
HALF = ROWS // 2
HALO = 16
TILE = 256
VROWS = HEAD_DIM + 16
PACK = LANES + 16
CHUNKS = 4
CCOLS = WIDTH // CHUNKS
NEG = -1e30
SCALE2 = HEAD_DIM ** -0.5 * 1.4426950408889634
FETCH_AT = 4
OPEN_AT = 0


def kernel(
    frames_in, taps_in, key_panel, value_panel, queries_in, offs_in,
    out,
    frames, taps, queries, offs, edge, xpad, wtap, score0, score1, prob0, prob1, enc, wbuf, kbuf, vbuf, hbuf, offown, offn, qn, bias, biasn,
    part, oret, pret, msend, ctx, stat, near,
    in_s, halo_s, halo_r, off_s, off_r, q_s, q_r, f_s, f_r,
    w_s, w_r, z_s, z_r, b_s, b_r, c_s, c_r, o_s, o_r, p_s, p_r,
):
    seq, mp = lax.axis_index("seq"), lax.axis_index("mp")
    me = seq * 8 + mp
    x, hi = mp // 2, mp % 2
    core, lo, kind = seq % 2, (seq // 2) % 2, (seq // 4) % 2
    sign = 1 - 2 * hi

    def at(index):
        wrapped = lax.rem(index + 256, 256)
        return {"seq": wrapped // 8, "mp": lax.rem(wrapped, 8)}

    up, down = at(me + 1), at(me - 1)
    partner = {"seq": seq, "mp": mp + sign}
    other = at(me - sign)
    onward = at(me + 2 * sign)
    source = at(me - 2 * sign)
    sibling = {"seq": seq + 1 - 2 * core, "mp": mp}
    across = {"seq": seq + 2 - 4 * lo, "mp": mp + sign}
    xplus = {"seq": seq, "mp": lax.rem(mp + 2, 8)}
    xminus = {"seq": seq, "mp": lax.rem(mp + 6, 8)}
    zplus = {"seq": lax.rem(seq + 4, 32), "mp": mp}
    zminus = {"seq": lax.rem(seq + 28, 32), "mp": mp}
    relay = {"seq": seq, "mp": lax.rem(mp + 6 + 4 * hi, 8)}

    def copy(src, dst, send, recv, device):
        return pltpu.make_async_remote_copy(
            src_ref=src, dst_ref=dst, send_sem=send, recv_sem=recv, device_id=device, device_id_type=MESH
        )

    def turn(step):
        return lax.rem(x + sign * step + 16, CHUNKS)

    def chunk_of(g):
        return turn(g + (g // 2) * (5 - 2 * g))

    def piece_of(g):
        return 2 * g + 2 * hi * ((g % 2) * (1 - g // 2) - (g // 2) * (1 - g % 2))

    slot_p, slot_o = 1 - hi, hi

    halo_up = copy(frames_in.at[pl.ds(ROWS - HALO, HALO)], hbuf.at[0], halo_s.at[0], halo_r.at[0], up)
    halo_down = copy(frames_in.at[pl.ds(0, HALO)], hbuf.at[1], halo_s.at[1], halo_r.at[1], down)
    off_p = copy(offown, offn.at[hi], off_s.at[0], off_r.at[hi], partner)
    off_o = copy(offown, offn.at[1 - hi], off_s.at[1], off_r.at[1 - hi], other)

    def q_copy(c):
        cols = pl.ds(c * CCOLS, CCOLS)
        return copy(queries_in.at[:, cols], qn.at[hi, :, cols], q_s.at[c], q_r.at[c], partner)

    def q_arrival(c):
        cols = pl.ds(c * CCOLS, CCOLS)
        dst = qn.at[slot_p, :, cols]
        return copy(dst, dst, q_s.at[c], q_r.at[c], partner)

    def f_copy(c):
        cols = pl.ds(c * CCOLS, CCOLS)
        return copy(qn.at[slot_p, :, cols], qn.at[hi, :, cols], f_s.at[c], f_r.at[c], onward)

    def f_arrival(c):
        cols = pl.ds(c * CCOLS, CCOLS)
        dst = qn.at[slot_o, :, cols]
        return copy(dst, dst, f_s.at[c], f_r.at[c], source)

    def piece(r, kv, half):
        return wbuf.at[r, kv, pl.ds(pl.multiple_of(half * HALF, HALF), HALF)]

    def w_copy(n, src, dst, device):
        return copy(piece(src, kind, core), piece(dst, kind, core), w_s.at[n], w_r.at[dst], device)

    own_across = w_copy(0, 0, 1, across)
    own_xplus = w_copy(1, 0, 4, xplus)
    own_xminus = w_copy(2, 0, 2, xminus)
    next_xplus = w_copy(3, 1, 5, xplus)
    next_xminus = w_copy(4, 1, 3, xminus)
    relay_own = w_copy(5, 2 + 2 * hi, 6, relay)
    relay_next = w_copy(6, 3 + 2 * hi, 7, relay)

    def w_arrival(r):
        dst = piece(r, kind, core)
        return copy(dst, dst, w_s.at[0], w_r.at[r], across)

    def z_copy(r, odd):
        src = piece(r, kind, core)
        return copy(src, src, z_s.at[r], z_r.at[r], zminus if odd else zplus)

    def z_arrival(r):
        dst = piece(r, 1 - kind, core)
        return copy(dst, dst, z_s.at[r], z_r.at[r], zplus)

    def b_copy(r):
        src = piece(r, kind, core)
        return copy(src, src, b_s.at[r], b_r.at[r], sibling)

    def b_arrival(r):
        dst = piece(r, kind, 1 - core)
        return copy(dst, dst, b_s.at[r], b_r.at[r], sibling)

    def c_copy(r):
        src = piece(r, 1 - kind, core)
        return copy(src, src, c_s.at[r], c_r.at[r], sibling)

    def c_arrival(r):
        dst = piece(r, 1 - kind, 1 - core)
        return copy(dst, dst, c_s.at[r], c_r.at[r], sibling)

    def fetched(r, odd):
        w_arrival(r).wait_recv()
        z_copy(r, odd).start()
        b_copy(r).start()

    def passed(r):
        z_arrival(r).wait_recv()
        c_copy(r).start()

    def onward_queries(c):
        q_arrival(c).wait_recv()
        f_copy(c).start()

    def o_copy(a):
        return copy(part.at[slot_o, a], oret.at[a], o_s.at[a], o_r.at[a], source)

    def p_copy(a):
        return copy(msend.at[a], pret.at[a], p_s.at[a], p_r.at[a], partner)

    barrier = pltpu.get_barrier_semaphore()
    greeted = (up, down, onward, source, sibling, across, xplus, xminus, zplus, zminus)
    for device in greeted:
        pl.semaphore_signal(barrier, inc=1, device_id=device, device_id_type=MESH)
    inputs = [
        pltpu.make_async_copy(src, dst, in_s.at[n])
        for n, (src, dst) in enumerate((
            (frames_in, frames), (taps_in, taps), (offs_in, offs),
            (key_panel, wbuf.at[0, 0]), (value_panel, wbuf.at[0, 1]), (queries_in, queries),
        ))
    ]
    for load in inputs:
        load.start()
    xpad[pl.ds(0, HALO), :] = jnp.zeros((HALO, LANES), F32)
    xpad[pl.ds(HALO + ROWS, HALO), :] = jnp.zeros((HALO, LANES), F32)
    for h in range(2):
        vbuf[:, h, HEAD_DIM:, :] = jnp.ones((BLOCKS, VROWS - HEAD_DIM, ROWS), BF)
    for load in inputs:
        load.wait()
    offown[...] = jnp.broadcast_to(offs[...], (8, TOKS))

    def open_up():
        pl.semaphore_wait(barrier, len(greeted))
        own_across.start()
        own_xplus.start()
        own_xminus.start()
        halo_up.start()
        halo_down.start()
        off_p.start()
        off_o.start()

    def band_bias(ref, first, row):
        count = ref.shape[0]

        def fill(n, _):
            rows = pl.ds(pl.multiple_of(n * 128, 128), 128)
            frame = first + n * 128 + lax.broadcasted_iota(jnp.int32, (128, TOKS), 0)
            gap = frame - row
            ref[rows, :] = jnp.where((gap & -BAND) == 0, 0.0, NEG)
            return 0

        lax.fori_loop(0, count // 128, fill, 0)

    band_bias(bias, me * ROWS, offown[0:1, :])

    def after_block(b):
        @pl.when(b == OPEN_AT)
        def _():
            open_up()

        @pl.when(b == FETCH_AT)
        def _():
            fetched(1, True)
            next_xplus.start()
            next_xminus.start()
            fetched(2 + 2 * hi, False)
            relay_own.start()
            fetched(4 - 2 * hi, False)
            for step in (0, -1, -2, -3):
                q_copy(turn(step)).start()

        @pl.when(b == 6)
        def _():
            passed(1)

        @pl.when(b == 7)
        def _():
            fetched(3 + 2 * hi, True)
            relay_next.start()
            fetched(5 - 2 * hi, True)
            onward_queries(turn(0))

    def convolve(source_ref, top, count, b):
        acc = jnp.zeros((count // 8, 8, LANES), F32)
        for phase in range(8):
            window = source_ref[pl.ds(top + phase + 1, count + 24), :].reshape(count // 8 + 3, 8, LANES)
            for k in range(phase, TAPS, 8):
                acc = acc + wtap[b, k] * window[k // 8 : k // 8 + count // 8]
        half = 0.5 * acc.reshape(count, LANES)
        here = source_ref[pl.ds(top + HALO, count), :]
        return (here + (half + half * jnp.tanh(half))).astype(BF)

    def conv_block(b, _):
        cols = pl.ds(pl.multiple_of(b * LANES, LANES), LANES)
        xpad[pl.ds(HALO, ROWS), :] = frames[:, cols].astype(F32)
        for k in range(TAPS):
            wtap[b, k] = jnp.broadcast_to(taps[pl.ds(k, 1), cols], (8, LANES))

        def tile(t, _):
            top = pl.multiple_of(t * TILE, TILE)
            enc[pl.ds(top, TILE), cols] = convolve(xpad, top, TILE, b)
            return 0

        lax.fori_loop(0, ROWS // TILE, tile, 0)
        after_block(b)
        return 0

    lax.fori_loop(0, BLOCKS, conv_block, 0)

    halo_up.wait_recv()
    halo_down.wait_recv()

    def edge_block(b, _):
        cols = pl.ds(pl.multiple_of(b * LANES, LANES), LANES)
        edge[0, :HALO, :] = jnp.where(me > 0, hbuf[0, :, cols].astype(F32), 0.0)
        edge[0, HALO:, :] = frames[: 2 * HALO, cols].astype(F32)
        edge[1, : 2 * HALO, :] = frames[ROWS - 2 * HALO :, cols].astype(F32)
        edge[1, 2 * HALO :, :] = jnp.where(me < 255, hbuf[1, :, cols].astype(F32), 0.0)
        enc[:HALO, cols] = convolve(edge.at[0], 0, HALO, b)
        enc[ROWS - HALO :, cols] = convolve(edge.at[1], 0, HALO, b)
        return 0

    lax.fori_loop(0, BLOCKS, edge_block, 0)

    for slot in range(2):
        copy(offn.at[slot], offn.at[slot], off_s.at[slot], off_r.at[slot], partner).wait_recv()
        band_bias(biasn.at[slot], me * ROWS + slot * HALF, offn[slot, 0:1, :])

    def project(r, a):
        weight = jnp.concatenate([wbuf[r, 0], wbuf[r, 1]], axis=1)
        both = jnp.dot(enc[...], weight, preferred_element_type=F32)
        kbuf[a] = both[:, :LANES].astype(BF)
        turned = both[:, LANES:].T.astype(BF)
        for h in range(2):
            vbuf[a, h, :HEAD_DIM, :] = turned[h * HEAD_DIM : (h + 1) * HEAD_DIM]

    def project_chunk(g):
        def one(k, _):
            r = piece_of(g) + k

            @pl.when(r > 0)
            def _():
                b_arrival(r).wait_recv()
                c_arrival(r).wait_recv()

            project(r, chunk_of(g) * 2 + lax.rem(hi + k, 2))
            return 0

        lax.fori_loop(0, 2, one, 0)

    lane = lax.broadcasted_iota(jnp.int32, (TOKS, LANES), 1)
    halves = (pl.ds(0, HALF), pl.ds(HALF, HALF))

    def head_queries(q, h):
        inside = (lane >= h * HEAD_DIM) & (lane < (h + 1) * HEAD_DIM)
        return jnp.where(inside, q.astype(F32), 0.0).astype(BF)

    def score(keys, q, h, mask, target):
        scores = lax.dot_general(
            keys, head_queries(q, h), (((1,), (1,)), ((), ())), preferred_element_type=F32
        ) + mask
        target[...] = scores
        return jnp.max(scores, axis=0, keepdims=True)

    def weigh(scores, peak, target):
        target[...] = jnp.exp2((scores[...] - peak) * SCALE2).astype(BF)

    def mix(values, weights):
        mixed = jnp.dot(values, weights, preferred_element_type=F32)
        return mixed[:HEAD_DIM], mixed[HEAD_DIM : HEAD_DIM + 1]

    score_refs, prob_refs = (score0, score1), (prob0, prob1)

    def three(v):
        first = v.astype(BF).astype(F32)
        second = (v - first).astype(BF).astype(F32)
        return [first, second, (v - first) - second]

    def panel_cols(a):
        return pl.ds(pl.multiple_of(a * LANES, LANES), LANES)

    def remote_score(a, h):
        return tuple(
            score(kbuf[a, halves[n], :], qn[n, :, panel_cols(a)], h, biasn[n], score_refs[h].at[halves[n]])
            for n in range(2)
        )

    def remote_weigh(h, peaks):
        for n in range(2):
            weigh(score_refs[h].at[halves[n]], peaks[n], prob_refs[h].at[halves[n]])

    def remote_mix(a, h, peaks):
        for n in range(2):
            mixed, total = mix(vbuf[a, h, :, halves[n]], prob_refs[h][halves[n], :])
            part[n, a, h * HEAD_DIM : (h + 1) * HEAD_DIM, :] = (mixed / total).astype(BF)
            rows = three(peaks[n]) + three(total) + [jnp.zeros((2, TOKS), F32)]
            stat[n, a, 8 * h : 8 * h + 8, :] = jnp.concatenate(rows, axis=0)

    def remote_pack(a):
        for n in range(2):
            part[n, a, LANES:, :] = stat[n, a].astype(BF)

    def merge(a):
        o_copy(a).wait_recv()
        theirs = oret[a].astype(F32)
        mine = part[slot_p, a].astype(F32)
        msend[a] = jnp.where(theirs[LANES : LANES + 1] > 0.1 * NEG, theirs, mine).astype(BF)
        p_copy(a).start()

    def merge_chunk(c):
        def one(k, _):
            merge(2 * c + k)
            return 0

        lax.fori_loop(0, 2, one, 0)

    def remote_chunk(c):
        peaks = remote_score(2 * c, 0)
        for k in range(2):
            a = 2 * c + k
            peaks1 = remote_score(a, 1)
            remote_weigh(0, peaks)
            remote_mix(a, 0, peaks)
            if k == 0:
                later = remote_score(a + 1, 0)
            remote_weigh(1, peaks1)
            remote_mix(a, 1, peaks1)
            remote_pack(a)
            o_copy(a).start()
            peaks = later

    def chunk_step(g, _):
        @pl.when(g == 0)
        def _():
            passed(2 + 2 * hi)
            passed(3 + 2 * hi)

        @pl.when(g == 1)
        def _():
            onward_queries(turn(-1))
            passed(4 - 2 * hi)
            passed(5 - 2 * hi)
            fetched(6, False)
            fetched(7, True)

        @pl.when(g == 2)
        def _():
            passed(6)
            passed(7)

        @pl.when(g < CHUNKS - 1)
        def _():
            project_chunk(g + 1)

        @pl.when(g == 0)
        def _():
            onward_queries(turn(2))

        f_arrival(chunk_of(g)).wait_recv()
        remote_chunk(chunk_of(g))

        @pl.when(g == 1)
        def _():
            merge_chunk(turn(1))

        @pl.when(g == 3)
        def _():
            merge_chunk(turn(0))
            merge_chunk(turn(2))

        return 0

    project_chunk(0)
    onward_queries(turn(1))
    lax.fori_loop(0, CHUNKS, chunk_step, 0)

    def own_score(a, h):
        return score(kbuf[a], queries[:, panel_cols(a)], h, bias[...], score_refs[h])

    def own_mix(a, h, peak):
        mixed, total = mix(vbuf[a, h], prob_refs[h][...])
        ctx[a, h * HEAD_DIM : (h + 1) * HEAD_DIM, :] = mixed
        near[a, 8 * h : 8 * h + 8, :] = jnp.concatenate([peak, total, jnp.zeros((6, TOKS), F32)], axis=0)

    def own_step(a, peak0):
        peak1 = own_score(a, 1)
        weigh(score0, peak0, prob0)
        own_mix(a, 0, peak0)
        peak_next = own_score(jnp.minimum(a + 1, BLOCKS - 1), 0)
        weigh(score1, peak1, prob1)
        own_mix(a, 1, peak1)

        @pl.when(a == 1)
        def _():
            merge_chunk(turn(-1))

        return peak_next

    lax.fori_loop(0, BLOCKS, own_step, own_score(0, 0))

    def final_step(a, _):
        cols = pl.ds(pl.multiple_of(a * LANES, LANES), LANES)
        p_copy(a).wait_recv()
        far_rows = pret[a, LANES:, :].astype(F32)
        parts = []
        for h in range(2):
            far_peak = sum(far_rows[8 * h + n : 8 * h + n + 1] for n in range(3))
            far_total = sum(far_rows[8 * h + n : 8 * h + n + 1] for n in range(3, 6))
            peak, total = near[a, 8 * h : 8 * h + 1, :], near[a, 8 * h + 1 : 8 * h + 2, :]
            top = jnp.maximum(peak, far_peak)
            near_weight = jnp.exp2((peak - top) * SCALE2)
            far_weight = jnp.exp2((far_peak - top) * SCALE2) * far_total
            scale = 1.0 / (near_weight * total + far_weight)
            head_rows = slice(h * HEAD_DIM, (h + 1) * HEAD_DIM)
            parts.append(
                ctx[a, head_rows, :] * (near_weight * scale) + pret[a, head_rows, :].astype(F32) * (far_weight * scale)
            )
        out[:, cols] = jnp.concatenate(parts, axis=0).T.astype(BF)
        return 0

    for step in (-1, 0, 2, 1):
        first = 2 * turn(step)
        lax.fori_loop(first, first + 2, final_step, 0)

    for sent in (
        halo_up, halo_down, off_p, off_o, own_across, own_xplus, own_xminus,
        next_xplus, next_xminus, relay_own, relay_next,
    ):
        sent.wait_send()
    for c in range(CHUNKS):
        q_copy(c).wait_send()
        f_copy(c).wait_send()

    for r in range(1, BLOCKS):
        z_copy(r, r % 2).wait_send()
        b_copy(r).wait_send()
        c_copy(r).wait_send()

    def drain(a, _):
        o_copy(a).wait_send()
        p_copy(a).wait_send()

        return 0

    lax.fori_loop(0, BLOCKS, drain, 0)


def shards(frames, conv_kernel, key_weight, value_weight, queries, offsets):
    dma = pltpu.SemaphoreType.DMA
    whole = pl.BlockSpec(memory_space=pltpu.VMEM)
    far = pl.BlockSpec(memory_space=pltpu.HBM)
    return pl.pallas_call(
        kernel,
        out_shape=jax.ShapeDtypeStruct((TOKS, WIDTH), BF),
        in_specs=[far] * 6,
        out_specs=whole,
        scratch_shapes=[
            pltpu.VMEM((ROWS, WIDTH), BF),
            pltpu.VMEM((TAPS, WIDTH), F32),
            pltpu.VMEM((TOKS, WIDTH), BF),
            pltpu.VMEM((1, TOKS), jnp.int32),
            pltpu.VMEM((2, 3 * HALO, LANES), F32),
            pltpu.VMEM((ROWS + 2 * HALO, LANES), F32),
            pltpu.VMEM((BLOCKS, TAPS, 8, LANES), F32),
            pltpu.VMEM((ROWS, TOKS), F32),
            pltpu.VMEM((ROWS, TOKS), F32),
            pltpu.VMEM((ROWS, TOKS), BF),
            pltpu.VMEM((ROWS, TOKS), BF),
            pltpu.VMEM((ROWS, WIDTH), BF),
            pltpu.VMEM((BLOCKS, 2, WIDTH, LANES), BF),
            pltpu.VMEM((BLOCKS, ROWS, LANES), BF),
            pltpu.VMEM((BLOCKS, 2, VROWS, ROWS), BF),
            pltpu.VMEM((2, HALO, WIDTH), BF),
            pltpu.VMEM((8, TOKS), jnp.int32),
            pltpu.VMEM((2, 8, TOKS), jnp.int32),
            pltpu.VMEM((2, TOKS, WIDTH), BF),
            pltpu.VMEM((ROWS, TOKS), F32),
            pltpu.VMEM((2, HALF, TOKS), F32),
            pltpu.VMEM((2, BLOCKS, PACK, TOKS), BF),
            pltpu.VMEM((BLOCKS, PACK, TOKS), BF),
            pltpu.VMEM((BLOCKS, PACK, TOKS), BF),
            pltpu.VMEM((BLOCKS, PACK, TOKS), BF),
            pltpu.VMEM((BLOCKS, LANES, TOKS), F32),
            pltpu.VMEM((2, BLOCKS, 16, TOKS), F32),
            pltpu.VMEM((BLOCKS, 16, TOKS), F32),
            dma((6,)), dma((2,)), dma((2,)), dma((2,)), dma((2,)),
            dma((CHUNKS,)), dma((CHUNKS,)), dma((CHUNKS,)), dma((CHUNKS,)),
            dma((7,)), dma((8,)), dma((8,)), dma((8,)), dma((8,)), dma((8,)), dma((8,)), dma((8,)),
            dma((BLOCKS,)), dma((BLOCKS,)), dma((BLOCKS,)), dma((BLOCKS,)),
        ],
        compiler_params=pltpu.CompilerParams(
            collective_id=0, has_side_effects=True, vmem_limit_bytes=63 * 1024 * 1024
        ),
        cost_estimate=pl.CostEstimate(
            flops=9_000_000_000, bytes_accessed=4_500_000, transcendentals=10_000_000
        ),
        name="speech_window",
    )(frames, conv_kernel, key_weight, value_weight, queries, offsets.reshape(1, TOKS))


def solution(mesh):
    return jax.shard_map(
        shards,
        mesh=mesh,
        in_specs=(
            P(("seq", "mp"), None),
            P(),
            P(None, "mp"),
            P(None, "mp"),
            P(("seq", "mp"), None),
            P(("seq", "mp")),
        ),
        out_specs=P(("seq", "mp"), None),
        check_vma=False,
    )
```

```python
import jax
import jax.numpy as jnp
from jax import lax
from jax.experimental import pallas as pl
from jax.experimental.pallas import tpu as pltpu
from jax.sharding import PartitionSpec as P

BF = jnp.bfloat16
F32 = jnp.float32
MESH = pl.DeviceIdType.MESH

HEAD_DIM = 64
BAND = 256
ROWS = 1024
TOKS = 256
WIDTH = 1024
LANES = 128
BLOCKS = WIDTH // LANES
TAPS = 31
HALF = ROWS // 2
HALO = 16
TILE = 256
VROWS = HEAD_DIM + 16
PACK = LANES + 16
CHUNKS = 4
CCOLS = WIDTH // CHUNKS
NEG = -1e30
SCALE2 = HEAD_DIM ** -0.5 * 1.4426950408889634
FETCH_AT = 3
EARLY_OWN = 0


def kernel(
    frames_in, taps_in, key_panel, value_panel, queries_in, offs_in,
    out,
    frames, taps, queries, offs, edge, xpad, wtap, score0, score1, prob0, prob1, enc, wbuf, kbuf, vbuf, hbuf, offown, offn, qn, bias, biasn,
    part, oret, pret, msend, ctx, stat, near,
    in_s, halo_s, halo_r, off_s, off_r, q_s, q_r, f_s, f_r,
    w_s, w_r, z_s, z_r, b_s, b_r, c_s, c_r, o_s, o_r, p_s, p_r,
):
    seq, mp = lax.axis_index("seq"), lax.axis_index("mp")
    me = seq * 8 + mp
    x, hi = mp // 2, mp % 2
    core, lo, kind = seq % 2, (seq // 2) % 2, (seq // 4) % 2
    sign = 1 - 2 * hi

    def at(index):
        wrapped = lax.rem(index + 256, 256)
        return {"seq": wrapped // 8, "mp": lax.rem(wrapped, 8)}

    up, down = at(me + 1), at(me - 1)
    partner = {"seq": seq, "mp": mp + sign}
    other = at(me - sign)
    onward = at(me + 2 * sign)
    source = at(me - 2 * sign)
    sibling = {"seq": seq + 1 - 2 * core, "mp": mp}
    across = {"seq": seq + 2 - 4 * lo, "mp": mp + sign}
    xplus = {"seq": seq, "mp": lax.rem(mp + 2, 8)}
    xminus = {"seq": seq, "mp": lax.rem(mp + 6, 8)}
    zplus = {"seq": lax.rem(seq + 4, 32), "mp": mp}
    zminus = {"seq": lax.rem(seq + 28, 32), "mp": mp}
    relay = {"seq": seq, "mp": lax.rem(mp + 6 + 4 * hi, 8)}

    def copy(src, dst, send, recv, device):
        return pltpu.make_async_remote_copy(
            src_ref=src, dst_ref=dst, send_sem=send, recv_sem=recv, device_id=device, device_id_type=MESH
        )

    def turn(step):
        return lax.rem(x + sign * step + 16, CHUNKS)

    def chunk_of(g):
        return turn(g + (g // 2) * (5 - 2 * g))

    def piece_of(g):
        return 2 * g + 2 * hi * ((g % 2) * (1 - g // 2) - (g // 2) * (1 - g % 2))

    slot_p, slot_o = 1 - hi, hi

    halo_up = copy(frames_in.at[pl.ds(ROWS - HALO, HALO)], hbuf.at[0], halo_s.at[0], halo_r.at[0], up)
    halo_down = copy(frames_in.at[pl.ds(0, HALO)], hbuf.at[1], halo_s.at[1], halo_r.at[1], down)
    off_p = copy(offown, offn.at[hi], off_s.at[0], off_r.at[hi], partner)
    off_o = copy(offown, offn.at[1 - hi], off_s.at[1], off_r.at[1 - hi], other)

    def q_copy(c):
        cols = pl.ds(c * CCOLS, CCOLS)
        return copy(queries_in.at[:, cols], qn.at[hi, :, cols], q_s.at[c], q_r.at[c], partner)

    def q_arrival(c):
        cols = pl.ds(c * CCOLS, CCOLS)
        dst = qn.at[slot_p, :, cols]
        return copy(dst, dst, q_s.at[c], q_r.at[c], partner)

    def f_copy(c):
        cols = pl.ds(c * CCOLS, CCOLS)
        return copy(qn.at[slot_p, :, cols], qn.at[hi, :, cols], f_s.at[c], f_r.at[c], onward)

    def f_arrival(c):
        cols = pl.ds(c * CCOLS, CCOLS)
        dst = qn.at[slot_o, :, cols]
        return copy(dst, dst, f_s.at[c], f_r.at[c], source)

    def piece(r, kv, half):
        return wbuf.at[r, kv, pl.ds(pl.multiple_of(half * HALF, HALF), HALF)]

    def w_copy(n, src, dst, device):
        return copy(piece(src, kind, core), piece(dst, kind, core), w_s.at[n], w_r.at[dst], device)

    own_across = w_copy(0, 0, 1, across)
    own_xplus = w_copy(1, 0, 4, xplus)
    own_xminus = w_copy(2, 0, 2, xminus)
    next_xplus = w_copy(3, 1, 5, xplus)
    next_xminus = w_copy(4, 1, 3, xminus)
    relay_own = w_copy(5, 2 + 2 * hi, 6, relay)
    relay_next = w_copy(6, 3 + 2 * hi, 7, relay)

    def w_arrival(r):
        dst = piece(r, kind, core)
        return copy(dst, dst, w_s.at[0], w_r.at[r], across)

    def z_copy(r, odd):
        src = piece(r, kind, core)
        return copy(src, src, z_s.at[r], z_r.at[r], zminus if odd else zplus)

    def z_arrival(r):
        dst = piece(r, 1 - kind, core)
        return copy(dst, dst, z_s.at[r], z_r.at[r], zplus)

    def b_copy(r):
        src = piece(r, kind, core)
        return copy(src, src, b_s.at[r], b_r.at[r], sibling)

    def b_arrival(r):
        dst = piece(r, kind, 1 - core)
        return copy(dst, dst, b_s.at[r], b_r.at[r], sibling)

    def c_copy(r):
        src = piece(r, 1 - kind, core)
        return copy(src, src, c_s.at[r], c_r.at[r], sibling)

    def c_arrival(r):
        dst = piece(r, 1 - kind, 1 - core)
        return copy(dst, dst, c_s.at[r], c_r.at[r], sibling)

    def fetched(r, odd):
        w_arrival(r).wait_recv()
        z_copy(r, odd).start()
        b_copy(r).start()

    def passed(r):
        z_arrival(r).wait_recv()
        c_copy(r).start()

    def onward_queries(c):
        q_arrival(c).wait_recv()
        f_copy(c).start()

    def o_copy(a):
        return copy(part.at[slot_o, a], oret.at[a], o_s.at[a], o_r.at[a], source)

    def p_copy(a):
        return copy(msend.at[a], pret.at[a], p_s.at[a], p_r.at[a], partner)

    barrier = pltpu.get_barrier_semaphore()
    greeted = (up, down, onward, source, sibling, across, xplus, xminus, zplus, zminus)
    for device in greeted:
        pl.semaphore_signal(barrier, inc=1, device_id=device, device_id_type=MESH)
    inputs = [
        pltpu.make_async_copy(src, dst, in_s.at[n])
        for n, (src, dst) in enumerate((
            (frames_in, frames), (taps_in, taps), (offs_in, offs),
            (key_panel, wbuf.at[0, 0]), (value_panel, wbuf.at[0, 1]), (queries_in, queries),
        ))
    ]
    for load in inputs:
        load.start()
    xpad[pl.ds(0, HALO), :] = jnp.zeros((HALO, LANES), F32)
    xpad[pl.ds(HALO + ROWS, HALO), :] = jnp.zeros((HALO, LANES), F32)
    for h in range(2):
        vbuf[:, h, HEAD_DIM:, :] = jnp.ones((BLOCKS, VROWS - HEAD_DIM, ROWS), BF)
    for load in inputs:
        load.wait()
    offown[...] = jnp.broadcast_to(offs[...], (8, TOKS))

    def open_up():
        pl.semaphore_wait(barrier, len(greeted))
        own_across.start()
        own_xplus.start()
        own_xminus.start()
        halo_up.start()
        halo_down.start()
        off_p.start()
        off_o.start()

    open_up()

    def band_bias(ref, first, row):
        count = ref.shape[0]

        def fill(n, _):
            rows = pl.ds(pl.multiple_of(n * 128, 128), 128)
            frame = first + n * 128 + lax.broadcasted_iota(jnp.int32, (128, TOKS), 0)
            gap = frame - row
            ref[rows, :] = jnp.where((gap & -BAND) == 0, 0.0, NEG)
            return 0

        lax.fori_loop(0, count // 128, fill, 0)

    band_bias(bias, me * ROWS, offown[0:1, :])

    def after_block(b):
        @pl.when(b == FETCH_AT)
        def _():
            fetched(1, True)
            next_xplus.start()
            next_xminus.start()
            fetched(2 + 2 * hi, False)
            relay_own.start()
            fetched(4 - 2 * hi, False)
            for step in (0, -1, -2, -3):
                q_copy(turn(step)).start()

        @pl.when(b == 6)
        def _():
            passed(1)

        @pl.when(b == 7)
        def _():
            fetched(3 + 2 * hi, True)
            relay_next.start()
            fetched(5 - 2 * hi, True)
            onward_queries(turn(0))

    def convolve(source_ref, top, count, b):
        acc = jnp.zeros((count // 8, 8, LANES), F32)
        for phase in range(8):
            window = source_ref[pl.ds(top + phase + 1, count + 24), :].reshape(count // 8 + 3, 8, LANES)
            for k in range(phase, TAPS, 8):
                acc = acc + wtap[b, k] * window[k // 8 : k // 8 + count // 8]
        half = 0.5 * acc.reshape(count, LANES)
        here = source_ref[pl.ds(top + HALO, count), :]
        return (here + (half + half * jnp.tanh(half))).astype(BF)

    def conv_block(b, _):
        cols = pl.ds(pl.multiple_of(b * LANES, LANES), LANES)
        xpad[pl.ds(HALO, ROWS), :] = frames[:, cols].astype(F32)
        for k in range(TAPS):
            wtap[b, k] = jnp.broadcast_to(taps[pl.ds(k, 1), cols], (8, LANES))

        def tile(t, _):
            top = pl.multiple_of(t * TILE, TILE)
            enc[pl.ds(top, TILE), cols] = convolve(xpad, top, TILE, b)
            return 0

        lax.fori_loop(0, ROWS // TILE, tile, 0)
        after_block(b)
        return 0

    lax.fori_loop(0, BLOCKS, conv_block, 0)

    halo_up.wait_recv()
    halo_down.wait_recv()

    def edge_block(b, _):
        cols = pl.ds(pl.multiple_of(b * LANES, LANES), LANES)
        edge[0, :HALO, :] = jnp.where(me > 0, hbuf[0, :, cols].astype(F32), 0.0)
        edge[0, HALO:, :] = frames[: 2 * HALO, cols].astype(F32)
        edge[1, : 2 * HALO, :] = frames[ROWS - 2 * HALO :, cols].astype(F32)
        edge[1, 2 * HALO :, :] = jnp.where(me < 255, hbuf[1, :, cols].astype(F32), 0.0)
        enc[:HALO, cols] = convolve(edge.at[0], 0, HALO, b)
        enc[ROWS - HALO :, cols] = convolve(edge.at[1], 0, HALO, b)
        return 0

    lax.fori_loop(0, BLOCKS, edge_block, 0)

    for slot in range(2):
        copy(offn.at[slot], offn.at[slot], off_s.at[slot], off_r.at[slot], partner).wait_recv()
        band_bias(biasn.at[slot], me * ROWS + slot * HALF, offn[slot, 0:1, :])

    def project(r, a):
        weight = jnp.concatenate([wbuf[r, 0], wbuf[r, 1]], axis=1)
        both = jnp.dot(enc[...], weight, preferred_element_type=F32)
        kbuf[a] = both[:, :LANES].astype(BF)
        turned = both[:, LANES:].T.astype(BF)
        for h in range(2):
            vbuf[a, h, :HEAD_DIM, :] = turned[h * HEAD_DIM : (h + 1) * HEAD_DIM]

    def project_chunk(g):
        def one(k, _):
            r = piece_of(g) + k

            @pl.when(r > 0)
            def _():
                b_arrival(r).wait_recv()
                c_arrival(r).wait_recv()

            project(r, chunk_of(g) * 2 + lax.rem(hi + k, 2))
            return 0

        lax.fori_loop(0, 2, one, 0)

    lane = lax.broadcasted_iota(jnp.int32, (TOKS, LANES), 1)
    halves = (pl.ds(0, HALF), pl.ds(HALF, HALF))

    def head_queries(q, h):
        inside = (lane >= h * HEAD_DIM) & (lane < (h + 1) * HEAD_DIM)
        return jnp.where(inside, q.astype(F32), 0.0).astype(BF)

    def score(keys, q, h, mask, target):
        scores = lax.dot_general(
            keys, head_queries(q, h), (((1,), (1,)), ((), ())), preferred_element_type=F32
        ) + mask
        target[...] = scores
        return jnp.max(scores, axis=0, keepdims=True)

    def weigh(scores, peak, target):
        target[...] = jnp.exp2((scores[...] - peak) * SCALE2).astype(BF)

    def mix(values, weights):
        mixed = jnp.dot(values, weights, preferred_element_type=F32)
        return mixed[:HEAD_DIM], mixed[HEAD_DIM : HEAD_DIM + 1]

    score_refs, prob_refs = (score0, score1), (prob0, prob1)

    def three(v):
        first = v.astype(BF).astype(F32)
        second = (v - first).astype(BF).astype(F32)
        return [first, second, (v - first) - second]

    def panel_cols(a):
        return pl.ds(pl.multiple_of(a * LANES, LANES), LANES)

    def remote_score(a, h):
        return tuple(
            score(kbuf[a, halves[n], :], qn[n, :, panel_cols(a)], h, biasn[n], score_refs[h].at[halves[n]])
            for n in range(2)
        )

    def remote_weigh(h, peaks):
        for n in range(2):
            weigh(score_refs[h].at[halves[n]], peaks[n], prob_refs[h].at[halves[n]])

    def remote_mix(a, h, peaks):
        for n in range(2):
            mixed, total = mix(vbuf[a, h, :, halves[n]], prob_refs[h][halves[n], :])
            part[n, a, h * HEAD_DIM : (h + 1) * HEAD_DIM, :] = (mixed / total).astype(BF)
            rows = three(peaks[n]) + three(total) + [jnp.zeros((2, TOKS), F32)]
            stat[n, a, 8 * h : 8 * h + 8, :] = jnp.concatenate(rows, axis=0)

    def remote_pack(a):
        for n in range(2):
            part[n, a, LANES:, :] = stat[n, a].astype(BF)

    def merge(a):
        o_copy(a).wait_recv()
        theirs = oret[a].astype(F32)
        mine = part[slot_p, a].astype(F32)
        msend[a] = jnp.where(theirs[LANES : LANES + 1] > 0.1 * NEG, theirs, mine).astype(BF)
        p_copy(a).start()

    def merge_chunk(c):
        def one(k, _):
            merge(2 * c + k)
            return 0

        lax.fori_loop(0, 2, one, 0)

    def remote_chunk(c):
        peaks = remote_score(2 * c, 0)
        for k in range(2):
            a = 2 * c + k
            peaks1 = remote_score(a, 1)
            remote_weigh(0, peaks)
            remote_mix(a, 0, peaks)
            if k == 0:
                later = remote_score(a + 1, 0)
            remote_weigh(1, peaks1)
            remote_mix(a, 1, peaks1)
            remote_pack(a)
            o_copy(a).start()
            peaks = later

    def own_score(a, h):
        return score(kbuf[a], queries[:, panel_cols(a)], h, bias[...], score_refs[h])

    def own_mix(a, h, peak):
        mixed, total = mix(vbuf[a, h], prob_refs[h][...])
        ctx[a, h * HEAD_DIM : (h + 1) * HEAD_DIM, :] = mixed
        near[a, 8 * h : 8 * h + 8, :] = jnp.concatenate([peak, total, jnp.zeros((6, TOKS), F32)], axis=0)

    def own_chunk(c):
        peak = own_score(2 * c, 0)
        for k in range(2):
            a = 2 * c + k
            peak1 = own_score(a, 1)
            weigh(score0, peak, prob0)
            own_mix(a, 0, peak)
            if k == 0:
                later = own_score(a + 1, 0)
            weigh(score1, peak1, prob1)
            own_mix(a, 1, peak1)
            peak = later

    def chunk_step(g, _):
        @pl.when(g == 0)
        def _():
            passed(2 + 2 * hi)
            passed(3 + 2 * hi)

        @pl.when(g == 1)
        def _():
            onward_queries(turn(-1))
            passed(6)
            passed(7)

        @pl.when(g < CHUNKS - 1)
        def _():
            project_chunk(g + 1)

        @pl.when(g == 0)
        def _():
            fetched(6, False)
            onward_queries(turn(2))
            passed(4 - 2 * hi)
            passed(5 - 2 * hi)
            fetched(7, True)

        @pl.when(g < EARLY_OWN)
        def _():
            own_chunk(chunk_of(g))

        @pl.when(g == 3)
        def _():
            merge_chunk(turn(0))

        f_arrival(chunk_of(g)).wait_recv()
        remote_chunk(chunk_of(g))

        @pl.when(g == 1)
        def _():
            merge_chunk(turn(1))

        @pl.when(g == 3)
        def _():
            merge_chunk(turn(2))

        return 0

    project_chunk(0)
    onward_queries(turn(1))
    lax.fori_loop(0, CHUNKS, chunk_step, 0)

    def late_own(g, _):
        own_chunk(chunk_of(g))

        @pl.when(g == EARLY_OWN)
        def _():
            merge_chunk(turn(-1))

        return 0

    lax.fori_loop(EARLY_OWN, CHUNKS, late_own, 0)


    def final_step(a, _):
        cols = pl.ds(pl.multiple_of(a * LANES, LANES), LANES)
        p_copy(a).wait_recv()
        far_rows = pret[a, LANES:, :].astype(F32)
        parts = []
        for h in range(2):
            far_peak = sum(far_rows[8 * h + n : 8 * h + n + 1] for n in range(3))
            far_total = sum(far_rows[8 * h + n : 8 * h + n + 1] for n in range(3, 6))
            peak, total = near[a, 8 * h : 8 * h + 1, :], near[a, 8 * h + 1 : 8 * h + 2, :]
            top = jnp.maximum(peak, far_peak)
            near_weight = jnp.exp2((peak - top) * SCALE2)
            far_weight = jnp.exp2((far_peak - top) * SCALE2) * far_total
            scale = 1.0 / (near_weight * total + far_weight)
            head_rows = slice(h * HEAD_DIM, (h + 1) * HEAD_DIM)
            parts.append(
                ctx[a, head_rows, :] * (near_weight * scale) + pret[a, head_rows, :].astype(F32) * (far_weight * scale)
            )
        out[:, cols] = jnp.concatenate(parts, axis=0).T.astype(BF)
        return 0

    for step in (-1, 0, 2, 1):
        first = 2 * turn(step)
        lax.fori_loop(first, first + 2, final_step, 0)

    for sent in (
        halo_up, halo_down, off_p, off_o, own_across, own_xplus, own_xminus,
        next_xplus, next_xminus, relay_own, relay_next,
    ):
        sent.wait_send()
    for c in range(CHUNKS):
        q_copy(c).wait_send()
        f_copy(c).wait_send()

    for r in range(1, BLOCKS):
        z_copy(r, r % 2).wait_send()
        b_copy(r).wait_send()
        c_copy(r).wait_send()

    def drain(a, _):
        o_copy(a).wait_send()
        p_copy(a).wait_send()

        return 0

    lax.fori_loop(0, BLOCKS, drain, 0)


def shards(frames, conv_kernel, key_weight, value_weight, queries, offsets):
    dma = pltpu.SemaphoreType.DMA
    whole = pl.BlockSpec(memory_space=pltpu.VMEM)
    far = pl.BlockSpec(memory_space=pltpu.HBM)
    return pl.pallas_call(
        kernel,
        out_shape=jax.ShapeDtypeStruct((TOKS, WIDTH), BF),
        in_specs=[far] * 6,
        out_specs=whole,
        scratch_shapes=[
            pltpu.VMEM((ROWS, WIDTH), BF),
            pltpu.VMEM((TAPS, WIDTH), F32),
            pltpu.VMEM((TOKS, WIDTH), BF),
            pltpu.VMEM((1, TOKS), jnp.int32),
            pltpu.VMEM((2, 3 * HALO, LANES), F32),
            pltpu.VMEM((ROWS + 2 * HALO, LANES), F32),
            pltpu.VMEM((BLOCKS, TAPS, 8, LANES), F32),
            pltpu.VMEM((ROWS, TOKS), F32),
            pltpu.VMEM((ROWS, TOKS), F32),
            pltpu.VMEM((ROWS, TOKS), BF),
            pltpu.VMEM((ROWS, TOKS), BF),
            pltpu.VMEM((ROWS, WIDTH), BF),
            pltpu.VMEM((BLOCKS, 2, WIDTH, LANES), BF),
            pltpu.VMEM((BLOCKS, ROWS, LANES), BF),
            pltpu.VMEM((BLOCKS, 2, VROWS, ROWS), BF),
            pltpu.VMEM((2, HALO, WIDTH), BF),
            pltpu.VMEM((8, TOKS), jnp.int32),
            pltpu.VMEM((2, 8, TOKS), jnp.int32),
            pltpu.VMEM((2, TOKS, WIDTH), BF),
            pltpu.VMEM((ROWS, TOKS), F32),
            pltpu.VMEM((2, HALF, TOKS), F32),
            pltpu.VMEM((2, BLOCKS, PACK, TOKS), BF),
            pltpu.VMEM((BLOCKS, PACK, TOKS), BF),
            pltpu.VMEM((BLOCKS, PACK, TOKS), BF),
            pltpu.VMEM((BLOCKS, PACK, TOKS), BF),
            pltpu.VMEM((BLOCKS, LANES, TOKS), F32),
            pltpu.VMEM((2, BLOCKS, 16, TOKS), F32),
            pltpu.VMEM((BLOCKS, 16, TOKS), F32),
            dma((6,)), dma((2,)), dma((2,)), dma((2,)), dma((2,)),
            dma((CHUNKS,)), dma((CHUNKS,)), dma((CHUNKS,)), dma((CHUNKS,)),
            dma((7,)), dma((8,)), dma((8,)), dma((8,)), dma((8,)), dma((8,)), dma((8,)), dma((8,)),
            dma((BLOCKS,)), dma((BLOCKS,)), dma((BLOCKS,)), dma((BLOCKS,)),
        ],
        compiler_params=pltpu.CompilerParams(
            collective_id=0, has_side_effects=True, vmem_limit_bytes=63 * 1024 * 1024
        ),
        cost_estimate=pl.CostEstimate(
            flops=9_000_000_000, bytes_accessed=4_500_000, transcendentals=10_000_000
        ),
        name="speech_window",
    )(frames, conv_kernel, key_weight, value_weight, queries, offsets.reshape(1, TOKS))


def solution(mesh):
    return jax.shard_map(
        shards,
        mesh=mesh,
        in_specs=(
            P(("seq", "mp"), None),
            P(),
            P(None, "mp"),
            P(None, "mp"),
            P(("seq", "mp"), None),
            P(("seq", "mp")),
        ),
        out_specs=P(("seq", "mp"), None),
        check_vma=False,
    )
```
